32 devices in a mesh: gx: 4 (over z), gy: 8 (over y, x, core).
Axes of the slice: x: 2, y: 2, z: 4, core: 2. Of those that a mesh axis runs over, the one named last changes fastest.
Arguments:
- position: float32 [3, 32, 64, 128], P(None, 'gx', 'gy'), may hold values from 0 to 1
- velocity: float32 [3, 32, 64, 128], P(None, 'gx', 'gy'), may hold values from -4 to 4
- history: float32 [3, 32, 64, 128], P(None, 'gx', 'gy'), may hold values from -4 to 4
- radius: float32 [32, 64, 128], P('gx', 'gy'), may hold values from 0.06 to 0.09
- fluid: float32 [3, 32, 64, 128], P(None, 'gx', 'gy'), may hold values from -6 to 6
- tile_list: int32 [32, 64, 4], P('gx', 'gy'), may hold values from 0 to 7, all different within a row
- tile_mask: int32 [32, 64, 4], P('gx', 'gy'), may hold values from 0 to 1
- move_slot: int32 [4, 32, 64, 64], P(None, 'gx', 'gy'), may hold values from 0 to 127, as said below
Outputs:
- position_out: float32 [3, 32, 64, 128], P(None, 'gx', 'gy')
- velocity_out: float32 [3, 32, 64, 128], P(None, 'gx', 'gy')
- history_out: float32 [3, 32, 64, 128], P(None, 'gx', 'gy')
The draws below stay inside these ranges and needn't reach their ends.
Inputs may be any that keep to these rules, and one draw needn't show every extreme that they name: `move_slot`: within a block and substep the 64 slots are distinct.
All inputs are finite; a program needn't handle non-finite values.
Results may differ from the reference program's by a relative error of at most 0.0003.
Values sent between devices are 32-bit elements; how exact they have to be, the bound alone decides.
A program may use at most 64 MiB of HBM per device.

```python
import math
import jax
import jax.numpy as jnp
import numpy as np
from jax import lax

GRAIN = 128
SUB = 4
NEAR = 4
MOVE = 16
NBX = 32
NBY = 64


def draw_tile_mask(key, part):
    key = jax.random.fold_in(key, 11)
    key_first, key_second, key_fill = jax.random.split(key, 3)
    centre_first = jax.random.randint(key_first, (), 0, NBX)
    centre_second = jax.random.randint(key_second, (), 0, NBY)
    row_ids = jnp.arange(NBX, dtype=jnp.int32)[:, None]
    col_ids = jnp.arange(NBY, dtype=jnp.int32)[None, :]
    spread = jnp.abs(row_ids - centre_first) + jnp.abs(col_ids - centre_second)
    level = jnp.maximum(2, 8 - 8 * spread // (NBX // 2 + NBY // 2 + 1))
    rolled = jax.random.randint(key_fill, (NBX, NBY, NEAR), 0, 8)
    return (rolled < level[:, :, None]).astype(jnp.int32)


def draw_move_slot(key, part):
    key = jax.random.fold_in(key, 7)
    blocks = SUB * NBX * NBY
    scores = jax.random.randint(key, (blocks, GRAIN), 0, 1 << 20)
    scores = scores * GRAIN + jnp.arange(GRAIN, dtype=jnp.int32)[None, :]
    order = jnp.argsort(scores, axis=1)
    return order[:, :4 * MOVE].reshape(SUB, NBX, NBY, 4 * MOVE).astype(jnp.int32)


def level_of(stream_key, extent, pieces, smallest, largest):
    def one(axis_at, blocks):
        steps = jax.random.uniform(jax.random.fold_in(jax.random.fold_in(stream_key, 6), axis_at), (blocks,), jnp.float32, smallest / len(pieces), largest / len(pieces))
        return jnp.repeat(jnp.exp(steps), extent[axis_at] // blocks).reshape((-1,) + (1,) * (len(extent) - axis_at - 1))

    level = one(*pieces[0])
    for cut in pieces[1:]:
        level = level * one(*cut)
    return level


def picks_of(own_key, rows, count, top, lift):
    ranking = jax.random.permutation(jax.random.fold_in(own_key, 1), count)
    favour = ranking
    for power in range(3):
        favour = favour * favour // count
    favour = favour * lift // count
    lots = jax.random.randint(jax.random.fold_in(own_key, 2), (rows, count), 0, 4096) + favour
    holders = jax.random.permutation(jax.random.fold_in(own_key, 3), rows)[jnp.arange(count) % rows]
    lots = jnp.where(jnp.arange(rows)[:, None] == holders[None, :], 1 << 14, lots)
    score = lots * count + jnp.arange(count)
    return lax.top_k(score.astype(jnp.int32), top)[1].astype(jnp.int32)


def scatter_about(stream_key, dims, scale, limit, shards=(), kind=jnp.bfloat16):
    values = scale * jax.random.normal(stream_key, dims, jnp.float32)
    if shards:
        values = values * level_of(stream_key, dims, shards, -0.22, 0.18)
    return jnp.clip(values, -limit, limit).astype(kind)


def setup_inputs(seed: int = 0) -> dict:
    seeds = jax.random.split(jax.random.key(seed), 9)
    position = jnp.clip(1.0 * jax.random.uniform(seeds[0], (3, NBX, NBY, GRAIN), jnp.float32) ** level_of(seeds[0], (3, NBX, NBY, GRAIN), ((1, 4), (2, 8)), -0.2, 0.2), 0.0, 1.0)
    velocity = scatter_about(seeds[1], (3, NBX, NBY, GRAIN), 0.5, 4.0, ((1, 4), (2, 8)), jnp.float32)
    history = scatter_about(seeds[2], (3, NBX, NBY, GRAIN), 0.5, 4.0, ((1, 4), (2, 8)), jnp.float32)
    radius = jnp.clip(jnp.exp(math.log(0.09) - 0.40546517 * jax.random.uniform(seeds[3], (NBX, NBY, GRAIN), jnp.float32) ** level_of(seeds[3], (NBX, NBY, GRAIN), ((0, 4), (1, 8)), -0.2, 0.2)), 0.06, 0.09)
    fluid = scatter_about(seeds[4], (3, NBX, NBY, GRAIN), 1.0, 6.0, ((1, 4), (2, 8)), jnp.float32)
    tile_list = picks_of(seeds[5], NBX * NBY, 8, NEAR, 0).reshape((NBX, NBY, NEAR))
    tile_mask = draw_tile_mask(jax.random.fold_in(seeds[8], 71), 0)
    move_slot = draw_move_slot(jax.random.fold_in(seeds[8], 71), 0)
    return {"position": position, "velocity": velocity, "history": history, "radius": radius, "fluid": fluid, "tile_list": tile_list, "tile_mask": tile_mask, "move_slot": move_slot}


time_step = 0.05
normal_stiff = 50.0
shear_stiff = 40.0
drag_rate = 2.0
gravity = 1.0
floor_square = 0.0025
base_radius = 0.075
shift_first = np.array([offset // 3 - 1 for offset in range(9)], np.float32)
shift_second = np.array([offset % 3 - 1 for offset in range(9)], np.float32)

def pair_forces(home, partner, offset_vec, weight, pair_mask):
    home_pos, home_his, home_rad = (home[0:3], home[3:6], home[6])
    far_pos, far_his, far_rad = (partner[0:3], partner[3:6], partner[6])
    delta = far_pos[:, :, None, :] + offset_vec[:, :, None, None] - home_pos[:, :, :, None]
    dist_sq = lax.optimization_barrier(jnp.sum(delta * delta, axis=0))
    distance = jnp.sqrt(jnp.maximum(dist_sq, floor_square))
    present = (far_rad > 0.0).astype(jnp.float32)
    intersection = jnp.maximum(home_rad[:, :, None] + far_rad[:, None, :] - distance, 0.0)
    intersection = intersection * present[:, None, :] * weight[:, None, None] * pair_mask
    pushing = lax.optimization_barrier(jnp.sum(intersection[None] * delta / distance[None], axis=3))
    loading = lax.optimization_barrier(jnp.sum(intersection, axis=2))
    spring = jnp.einsum('bij,cbj->cbi', intersection, far_his, precision=lax.Precision.HIGHEST)
    return -normal_stiff * pushing - shear_stiff * (home_his * loading[None] - spring)

def row_force(window, tile_row, mask_row):
    home = window[:, 1, 1:-1]
    width = home.shape[1]
    grains = home.shape[2]
    views = jnp.stack([window[:, offset // 3, offset % 3:offset % 3 + width] for offset in range(9)])
    zero_vec = jnp.zeros((3, width), jnp.float32)
    self_mask = 1.0 - jnp.eye(grains, dtype=jnp.float32)
    total = pair_forces(home, home, zero_vec, jnp.ones((width,), jnp.float32), self_mask)
    picked = tile_row + (tile_row >= 4).astype(jnp.int32)
    onehot = (picked[:, :, None] == jnp.arange(9, dtype=jnp.int32)[None, None, :]).astype(jnp.float32)
    weights = mask_row.astype(jnp.float32)
    for slot_k in range(tile_row.shape[1]):
        select = onehot[:, slot_k].T
        partner = lax.optimization_barrier(jnp.sum(select[:, None, :, None] * views, axis=0))
        along_one = lax.optimization_barrier(jnp.sum(select * jnp.asarray(shift_first)[:, None], axis=0))
        along_two = lax.optimization_barrier(jnp.sum(select * jnp.asarray(shift_second)[:, None], axis=0))
        offset_vec = jnp.stack([along_one, along_two, jnp.zeros_like(along_one)])
        total = total + pair_forces(home, partner, offset_vec, weights[:, slot_k], 1.0)
    return total

def all_forces(padded, tile_list, tile_mask):
    rows = padded.shape[1] - 2

    def one_row(row_index):
        window = lax.dynamic_slice_in_dim(padded, row_index, 3, axis=1)
        return row_force(window, tile_list[row_index], tile_mask[row_index])
    result = lax.map(one_row, jnp.arange(rows, dtype=jnp.int32))
    return jnp.moveaxis(result, 0, 1)

def advance(position, velocity, history, radius, fluid, force):
    vertical = jnp.array([0.0, 0.0, 1.0], jnp.float32).reshape(3, 1, 1, 1)
    lift = normal_stiff * jnp.maximum(radius - position[2], 0.0)
    force = force + lift[None] * vertical
    mass = (radius / base_radius) ** 3
    accel = force / mass[None] + drag_rate * (fluid - velocity) - gravity * vertical
    velocity = velocity + time_step * accel
    history = history + time_step * velocity
    position = position + time_step * velocity
    return (position, velocity, history)

def place(state, slots, values):
    row_ids = jnp.arange(slots.shape[0], dtype=jnp.int32)[:, None, None]
    col_ids = jnp.arange(slots.shape[1], dtype=jnp.int32)[None, :, None]
    return state.at[:, row_ids, col_ids, slots].set(values)

def unit_channel(which):
    return (jnp.arange(10) == which).astype(jnp.float32).reshape(10, 1, 1, 1)

def migrate(state, slots):
    count = slots.shape[-1] // 4
    groups = [slots[..., part_k * count:(part_k + 1) * count] for part_k in range(4)]
    packets = [jnp.take_along_axis(state, group[None], axis=3) for group in groups]
    first_unit = unit_channel(0)
    second_unit = unit_channel(1)
    into_minus_x = jnp.concatenate([packets[1][:, :1], packets[0][:, :-1] - first_unit], axis=1)
    into_plus_x = jnp.concatenate([packets[1][:, 1:] + first_unit, packets[0][:, -1:]], axis=1)
    into_minus_y = jnp.concatenate([packets[3][:, :, :1], packets[2][:, :, :-1] - second_unit], axis=2)
    into_plus_y = jnp.concatenate([packets[3][:, :, 1:] + second_unit, packets[2][:, :, -1:]], axis=2)
    state = place(state, groups[1], into_minus_x)
    state = place(state, groups[0], into_plus_x)
    state = place(state, groups[3], into_minus_y)
    state = place(state, groups[2], into_plus_y)
    return state

def reference(position, velocity, history, radius, fluid, tile_list, tile_mask, move_slot):
    for step_no in range(move_slot.shape[0]):
        ghost = jnp.concatenate([position, history, radius[None]], axis=0)
        padded = jnp.pad(ghost, ((0, 0), (1, 1), (1, 1), (0, 0)))
        force = all_forces(padded, tile_list, tile_mask)
        position, velocity, history = advance(position, velocity, history, radius, fluid, force)
        state = jnp.concatenate([position, velocity, history, radius[None]], axis=0)
        state = migrate(state, move_slot[step_no])
        position, velocity, history, radius = (state[0:3], state[3:6], state[6:9], state[9])
    return (position, velocity, history)
```

```python
import functools

import jax
import jax.numpy as jnp
from jax import lax
from jax.experimental import pallas as pl
from jax.experimental.pallas import tpu as pltpu
from jax.sharding import PartitionSpec as P

time_step = 0.05
normal_stiff = 50.0
shear_stiff = 40.0
drag_rate = 2.0
gravity = 1.0
floor_square = 0.0025
base_radius = 0.075
centre = 0.5
absent = -1.0e9
TILE = 16
MESH = pl.DeviceIdType.MESH
f32 = jnp.float32
bf16 = jnp.bfloat16


def pieces(x):
    high = x.astype(bf16).astype(f32)
    rest = x - high
    mid = rest.astype(bf16).astype(f32)
    low = (rest - mid).astype(bf16).astype(f32)
    return high, mid, low


def kernel(
    sizes, pos, vel, his, rad, fluid, slot, inv, listed, masked, pos_out, vel_out, his_out,
    state, packet, left, value, radb, drag, send_edge, land_edge, send_corner, land_corner,
    send_sem, recv_sem,
):
    size_x, size_y, rows, cols, steps, near = sizes
    wide = cols + 2
    high = rows + 2
    me_x = lax.axis_index("gx")
    me_y = lax.axis_index("gy")
    ahead_x, behind_x = lax.rem(me_x + 1, size_x), lax.rem(me_x + size_x - 1, size_x)
    ahead_y, behind_y = lax.rem(me_y + 1, size_y), lax.rem(me_y + size_y - 1, size_y)
    targets = [
        (ahead_x, me_y), (behind_x, me_y), (me_x, ahead_y), (me_x, behind_y),
        (ahead_x, ahead_y), (ahead_x, behind_y), (behind_x, ahead_y), (behind_x, behind_y),
    ]
    has_ahead_x, has_behind_x = me_x < size_x - 1, me_x > 0
    has_ahead_y, has_behind_y = me_y < size_y - 1, me_y > 0

    barrier = pltpu.get_barrier_semaphore()
    for target in targets:
        pl.semaphore_signal(barrier, inc=1, device_id=target, device_id_type=MESH)

    row8 = lax.broadcasted_iota(jnp.int32, (8, 128), 0)

    def load_row(a, _):
        first = ((a + 1) * wide + 1) * TILE
        for c in range(3):
            state[pl.ds(first + c, cols, stride=TILE), :] = pos[c, a]
            state[pl.ds(first + 5 + c, cols, stride=TILE), :] = his[c, a]
            state[pl.ds(first + 8 + c, cols, stride=TILE), :] = vel[c, a]
            drag[pl.ds(a * cols * 8 + c, cols, stride=8), :] = fluid[c, a]
        state[pl.ds(first + 3, cols, stride=TILE), :] = rad[a]
        zero = jnp.zeros((cols, 128), f32)
        for c in (4, 11, 12, 13, 14, 15):
            state[pl.ds(first + c, cols, stride=TILE), :] = zero
        return 0

    lax.fori_loop(0, rows, load_row, 0)

    def copies(x):
        out = []
        for d in range(8):
            source, landing, k = (
                (send_edge, land_edge, d) if d < 4 else (send_corner, land_corner, d - 4)
            )
            out.append(
                pltpu.make_async_remote_copy(
                    src_ref=source.at[x, k],
                    dst_ref=landing.at[x, k],
                    send_sem=send_sem.at[x, d],
                    recv_sem=recv_sem.at[x, d],
                    device_id=targets[d],
                    device_id_type=MESH,
                )
            )
        return out

    def block(r, c):
        return pl.ds(pl.multiple_of((r * wide + c) * TILE, TILE), TILE)

    def run(r, c, count):
        return pl.ds(pl.multiple_of((r * wide + c) * TILE, TILE), count * TILE)

    def send(x):
        send_edge[x, 0] = state[run(rows, 1, cols), :]
        send_edge[x, 1] = state[run(1, 1, cols), :]
        for r in range(rows):
            send_edge[x, 2, r * TILE : (r + 1) * TILE] = state[block(r + 1, cols), :]
            send_edge[x, 3, r * TILE : (r + 1) * TILE] = state[block(r + 1, 1), :]
        send_corner[x, 0] = state[block(rows, cols), :]
        send_corner[x, 1] = state[block(rows, 1), :]
        send_corner[x, 2] = state[block(1, cols), :]
        send_corner[x, 3] = state[block(1, 1), :]
        for copy in copies(x):
            copy.start()

    def receive(x):
        for copy in copies(x):
            copy.wait_recv()
        ax, bx = has_ahead_x.astype(f32), has_behind_x.astype(f32)
        ay, by = has_ahead_y.astype(f32), has_behind_y.astype(f32)
        state[run(0, 1, cols), :] = land_edge[x, 0] * bx
        state[run(rows + 1, 1, cols), :] = land_edge[x, 1] * ax
        for r in range(rows):
            state[block(r + 1, 0), :] = land_edge[x, 2, r * TILE : (r + 1) * TILE] * by
            state[block(r + 1, cols + 1), :] = land_edge[x, 3, r * TILE : (r + 1) * TILE] * ay
        state[block(0, 0), :] = land_corner[x, 0] * (bx * by)
        state[block(0, cols + 1), :] = land_corner[x, 1] * (bx * ay)
        state[block(rows + 1, 0), :] = land_corner[x, 2] * (ax * by)
        state[block(rows + 1, cols + 1), :] = land_corner[x, 3] * (ax * ay)

    pl.semaphore_wait(barrier, 8)
    send(0)
    receive(0)

    def features(n):
        tile = state[pl.ds(pl.multiple_of(n * TILE, TILE), 8), :]
        x = jnp.where(row8 < 3, tile - centre, tile)
        norm = jnp.sum(jnp.where(row8 < 3, x * x, 0.0), axis=0, keepdims=True)
        radius = tile[3:4]
        x = jnp.where(row8 == 3, norm, jnp.where(row8 == 4, 1.0, x))
        h, m, l = pieces(x)
        zero = jnp.zeros_like(h)
        seen = jnp.where(row8 == 0, jnp.where(radius > 0.0, radius, absent), 0.0)
        turned = jnp.transpose(
            jnp.concatenate([h, h, m, h, l, m, zero, zero, seen] + [zero] * 7, axis=0)
        )
        left[n] = turned.astype(bf16)
        radb[n] = jnp.broadcast_to(turned[:, 64:65], (128, 128))
        v = jnp.concatenate([h, m, l, zero], axis=0).astype(bf16)
        value[n] = jnp.concatenate([v, v], axis=1)

    def pair_sums(m, home, u, v, row_radius):
        x = home - jnp.where(row8 == 0, u, jnp.where(row8 == 1, v, 0.0))
        norm = jnp.sum(jnp.where(row8 < 3, x * x, 0.0), axis=0, keepdims=True)
        y = jnp.where(
            row8 < 3, -2.0 * x, jnp.where(row8 == 3, 1.0, jnp.where(row8 == 4, norm, 0.0))
        )
        h, mid, l = pieces(y)
        zero = jnp.zeros_like(h)
        right = jnp.concatenate([h, mid, h, l, h, mid, zero, zero], axis=0).astype(bf16)
        square = jnp.dot(left[m][:, 0:64], right, preferred_element_type=f32)
        square = jnp.maximum(square, floor_square)
        over = lax.rsqrt(square)
        s = jnp.maximum((radb[m] + row_radius) - square * over, 0.0)
        q = s * over
        s_high, q_high = s.astype(bf16), q.astype(bf16)
        s_low = (s - s_high.astype(f32)).astype(bf16)
        q_low = (q - q_high.astype(f32)).astype(bf16)
        weights = jnp.concatenate(
            [
                jnp.concatenate([s_high, q_high], axis=1),
                jnp.concatenate([s_low, q_low], axis=1),
            ],
            axis=0,
        )
        sums = jnp.dot(
            value[m], weights, preferred_element_type=f32
        )
        sums = sums[0:8] + sums[8:16] + sums[16:24]
        picked = jnp.where(row8 < 4, sums[:, 128:], sums[:, :128])
        total = jnp.where(row8 < 4, sums[4:5, 128:], sums[4:5, :128])
        return picked - x * total

    def advance(step, a, b):
        n = (a + 1) * wide + b + 1
        here = pl.ds(pl.multiple_of(n * TILE, TILE), TILE)
        tile = state[here, :]
        home = jnp.where(row8 < 3, tile[0:8] - centre, tile[0:8])
        radius = tile[3:4]
        acc = pair_sums(n, home, 0.0, 0.0, radius)
        for e in range(near):
            at = (a * cols + b) * near + e
            picked = listed[at]
            offset = jnp.where(picked >= 4, picked + 1, picked)
            u = jnp.where(offset >= 6, 1, jnp.where(offset >= 3, 0, -1))
            v = offset - 3 * (u + 1) - 1
            row_radius = radius + jnp.where(masked[at] > 0, 0.0, absent)
            acc = acc + pair_sums(
                n + u * wide + v, home, u.astype(f32), v.astype(f32), row_radius
            )
        force = -normal_stiff * acc[0:3] + shear_stiff * acc[5:8]
        lift = normal_stiff * jnp.maximum(radius - tile[2:3], 0.0)
        row3 = lax.broadcasted_iota(jnp.int32, (3, 128), 0)
        force = force + jnp.where(row3 == 2, lift, 0.0)
        ratio = radius / base_radius
        speed = tile[8:11]
        wind = drag[pl.ds(pl.multiple_of((a * cols + b) * 8, 8), 8), :][0:3]
        accel = (
            force / (ratio * ratio * ratio)
            + drag_rate * (wind - speed)
            - jnp.where(row3 == 2, gravity, 0.0)
        )
        speed = speed + time_step * accel
        moved = tile[0:3] + time_step * speed
        spring = tile[5:8] + time_step * speed
        back = inv[step, a, pl.ds(b, 1), :].astype(f32)
        slots = slot[step, a, pl.ds(b, 1), :].astype(f32)
        state[here, :] = jnp.concatenate(
            [moved, radius, back, spring, speed, slots, tile[12:16]], axis=0
        )

    def spread(rows_of, count):
        one = rows_of.reshape(count, 1, 128)
        return jnp.broadcast_to(one, (count, TILE, 128))

    def make_packets(r, c, count):
        tiles = state[run(r, c, count), :].reshape(count, TILE, 128)
        index = spread(tiles[:, 11:12, :], count).astype(jnp.int32).reshape(count * TILE, 128)
        packet[run(r, c, count), :] = jnp.take_along_axis(
            tiles.reshape(count * TILE, 128), index, axis=1, mode="promise_in_bounds"
        )

    def trade(r, c, count, open_x, open_y):
        shape = (count, TILE, 128)
        up = packet[run(jnp.minimum(r + 1, high - 1), c, count), :].reshape(shape)
        down = packet[run(jnp.maximum(r - 1, 0), c, count), :].reshape(shape)
        if c == 0:
            line = packet[run(r, 0, count), :].reshape(shape)
            ahead = jnp.concatenate([line[1:], line[:1]], axis=0)
            behind = jnp.concatenate([line[-1:], line[:-1]], axis=0)
        else:
            ahead = packet[run(r, c + 1, count), :].reshape(shape)
            behind = packet[run(r, c - 1, count), :].reshape(shape)
        lane = lax.broadcasted_iota(jnp.int32, shape, 2)
        line_no = lax.broadcasted_iota(jnp.int32, shape, 1)
        column = lax.broadcasted_iota(jnp.int32, shape, 0) + c
        shift = jnp.where(
            lane < 32,
            jnp.where(line_no == 0, jnp.where(lane < 16, 1.0, -1.0), 0.0),
            jnp.where(line_no == 1, jnp.where(lane < 48, 1.0, -1.0), 0.0),
        )
        arriving = jnp.where(
            lane < 32, jnp.where(lane < 16, up, down), jnp.where(lane < 48, ahead, behind)
        )
        arriving = (arriving + shift).reshape(count * TILE, 128)
        tiles = state[run(r, c, count), :].reshape(shape)
        back = spread(tiles[:, 4:5, :], count).astype(jnp.int32)
        index = jnp.maximum(back, 0).reshape(count * TILE, 128)
        found = jnp.take_along_axis(arriving, index, axis=1, mode="promise_in_bounds")
        flag_y0, flag_y1 = open_y(column)
        allowed = jnp.where(
            back < 32,
            jnp.where(back < 16, open_x[0], open_x[1]),
            jnp.where(back < 48, flag_y0, flag_y1),
        )
        allowed = jnp.where((back >= 0) & (line_no != 4) & (line_no != 11), allowed, 0)
        state[run(r, c, count), :] = jnp.where(
            allowed > 0, found.reshape(shape), tiles
        ).reshape(count * TILE, 128)

    def as_int(flag):
        return jnp.where(flag, 1, 0)

    def substep(step, _):
        def feature_row(r, _):
            for c in range(wide):
                features(r * wide + c)
            return 0

        lax.fori_loop(0, high, feature_row, 0)

        def advance_one(i, _):
            a = i // cols
            advance(step, a, i - a * cols)
            return 0

        lax.fori_loop(0, rows * cols, advance_one, 0)

        def packets_row(r, _):
            make_packets(r, 1, cols)
            return 0

        lax.fori_loop(1, rows + 1, packets_row, 0)

        def inner_row(r, _):
            trade(
                r, 1, cols, (as_int(r < rows), as_int(r > 1)),
                lambda column: (as_int(column < cols), as_int(column > 1)),
            )
            return 0

        lax.fori_loop(1, rows + 1, inner_row, 0)
        send(step + 1)
        receive(step + 1)
        make_packets(0, 0, wide)
        make_packets(rows + 1, 0, wide)

        def side_row(r, _):
            make_packets(r, 0, 1)
            make_packets(r, cols + 1, 1)
            return 0

        lax.fori_loop(1, rows + 1, side_row, 0)
        behind_x_open, ahead_x_open = as_int(has_behind_x), as_int(has_ahead_x)
        behind_y_open, ahead_y_open = as_int(has_behind_y), as_int(has_ahead_y)

        def cross_row(r, _):
            plus = jnp.where(r == 0, behind_x_open, jnp.where(r == rows, ahead_x_open, 0))
            minus = jnp.where(r == 1, behind_x_open, jnp.where(r == rows + 1, ahead_x_open, 0))

            def open_y(column):
                return (
                    jnp.where(
                        column == 0, behind_y_open, jnp.where(column == cols, ahead_y_open, 0)
                    ),
                    jnp.where(
                        column == 1, behind_y_open, jnp.where(column == cols + 1, ahead_y_open, 0)
                    ),
                )

            trade(r, 0, wide, (plus, minus), open_y)
            return 0

        lax.fori_loop(0, high, cross_row, 0)
        return 0

    lax.fori_loop(0, steps, substep, 0)

    def store_row(a, _):
        first = ((a + 1) * wide + 1) * TILE
        for c in range(3):
            pos_out[c, a] = state[pl.ds(first + c, cols, stride=TILE), :]
            his_out[c, a] = state[pl.ds(first + 5 + c, cols, stride=TILE), :]
            vel_out[c, a] = state[pl.ds(first + 8 + c, cols, stride=TILE), :]
        return 0

    lax.fori_loop(0, rows, store_row, 0)

    def drain(x, _):
        for copy in copies(x):
            copy.wait_send()
        return 0

    lax.fori_loop(0, steps + 1, drain, 0)


def on_device(position, velocity, history, radius, fluid, tile_list, tile_mask, move_slot):
    size_x, size_y = lax.axis_size("gx"), lax.axis_size("gy")
    rows, cols, grains = radius.shape
    steps, near = move_slot.shape[0], tile_list.shape[-1]
    count = move_slot.shape[-1] // 4
    order = jnp.arange(4 * count, dtype=jnp.int32)
    hit = move_slot[..., :, None] == jnp.arange(grains, dtype=jnp.int32)
    inverse = jnp.sum(jnp.where(hit, order[:, None] + 1, 0), axis=-2) - 1
    groups = [move_slot[..., k * count : (k + 1) * count] for k in (1, 0, 3, 2)]
    slots = jnp.concatenate(groups + [jnp.zeros_like(move_slot)], axis=-1)
    blocks = (rows + 2) * (cols + 2)
    shape = jax.ShapeDtypeStruct(position.shape, f32)
    vmem = pl.BlockSpec(memory_space=pltpu.VMEM)
    smem = pl.BlockSpec(memory_space=pltpu.SMEM)
    return pl.pallas_call(
        functools.partial(kernel, (size_x, size_y, rows, cols, steps, near)),
        out_shape=(shape, shape, shape),
        in_specs=[vmem] * 7 + [smem] * 2,
        out_specs=(vmem, vmem, vmem),
        scratch_shapes=[
            pltpu.VMEM((blocks * TILE, grains), f32),
            pltpu.VMEM((blocks * TILE, grains), f32),
            pltpu.VMEM((blocks, 128, 128), bf16),
            pltpu.VMEM((blocks, 32, 256), bf16),
            pltpu.VMEM((blocks, 128, 128), f32),
            pltpu.VMEM((rows * cols * 8, grains), f32),
            pltpu.VMEM((steps + 1, 4, max(rows, cols) * TILE, grains), f32),
            pltpu.VMEM((steps + 1, 4, max(rows, cols) * TILE, grains), f32),
            pltpu.VMEM((steps + 1, 4, TILE, grains), f32),
            pltpu.VMEM((steps + 1, 4, TILE, grains), f32),
            pltpu.SemaphoreType.DMA((steps + 1, 8)),
            pltpu.SemaphoreType.DMA((steps + 1, 8)),
        ],
        compiler_params=pltpu.CompilerParams(
            collective_id=0, has_side_effects=True, vmem_limit_bytes=40 * 1024 * 1024
        ),
    )(
        position, velocity, history, radius, fluid, slots, inverse,
        tile_list.reshape(-1), tile_mask.reshape(-1),
    )


def solution(mesh):
    grid = P(None, "gx", "gy", None)
    flat = P("gx", "gy", None)
    return jax.shard_map(
        on_device,
        mesh=mesh,
        in_specs=(grid, grid, grid, flat, grid, flat, flat, grid),
        out_specs=(grid, grid, grid),
        check_vma=False,
    )
```

```python
import functools

import jax
import jax.numpy as jnp
from jax import lax
from jax.experimental import pallas as pl
from jax.experimental.pallas import tpu as pltpu
from jax.sharding import PartitionSpec as P

time_step = 0.05
normal_stiff = 50.0
shear_stiff = 40.0
drag_rate = 2.0
gravity = 1.0
floor_square = 0.0025
base_radius = 0.075
centre = 0.5
absent = -1.0e9
TILE = 16
MESH = pl.DeviceIdType.MESH
f32 = jnp.float32
bf16 = jnp.bfloat16


def pieces(x):
    high = x.astype(bf16).astype(f32)
    rest = x - high
    mid = rest.astype(bf16).astype(f32)
    low = (rest - mid).astype(bf16).astype(f32)
    return high, mid, low


def kernel(
    sizes, pos, vel, his, rad, fluid, slot, inv, listed, masked, pos_out, vel_out, his_out,
    state, packet, left, value, radb, drag, send_edge, land_edge, send_corner, land_corner,
    send_sem, recv_sem,
):
    size_x, size_y, rows, cols, steps, near = sizes
    wide = cols + 2
    high = rows + 2
    me_x = lax.axis_index("gx")
    me_y = lax.axis_index("gy")
    ahead_x, behind_x = lax.rem(me_x + 1, size_x), lax.rem(me_x + size_x - 1, size_x)
    ahead_y, behind_y = lax.rem(me_y + 1, size_y), lax.rem(me_y + size_y - 1, size_y)
    targets = [
        (ahead_x, me_y), (behind_x, me_y), (me_x, ahead_y), (me_x, behind_y),
        (ahead_x, ahead_y), (ahead_x, behind_y), (behind_x, ahead_y), (behind_x, behind_y),
    ]
    has_ahead_x, has_behind_x = me_x < size_x - 1, me_x > 0
    has_ahead_y, has_behind_y = me_y < size_y - 1, me_y > 0

    barrier = pltpu.get_barrier_semaphore()
    present = [
        has_ahead_x, has_behind_x, has_ahead_y, has_behind_y,
        has_ahead_x & has_ahead_y, has_ahead_x & has_behind_y,
        has_behind_x & has_ahead_y, has_behind_x & has_behind_y,
    ]
    opposite = [1, 0, 3, 2, 7, 6, 5, 4]
    for target, there in zip(targets, present):

        @pl.when(there)
        def _():
            pl.semaphore_signal(barrier, inc=1, device_id=target, device_id_type=MESH)


    row8 = lax.broadcasted_iota(jnp.int32, (8, 128), 0)

    def load_row(a, _):
        first = ((a + 1) * wide + 1) * TILE
        for c in range(3):
            state[pl.ds(first + c, cols, stride=TILE), :] = pos[c, a]
            state[pl.ds(first + 5 + c, cols, stride=TILE), :] = his[c, a]
            state[pl.ds(first + 8 + c, cols, stride=TILE), :] = vel[c, a]
            drag[pl.ds(a * cols * 8 + c, cols, stride=8), :] = fluid[c, a]
        state[pl.ds(first + 3, cols, stride=TILE), :] = rad[a]
        zero = jnp.zeros((cols, 128), f32)
        for c in (4, 11, 12, 13, 14, 15):
            state[pl.ds(first + c, cols, stride=TILE), :] = zero
        return 0

    lax.fori_loop(0, rows, load_row, 0)

    def copies(x):
        out = []
        for d in range(8):
            source, landing, k = (
                (send_edge, land_edge, d) if d < 4 else (send_corner, land_corner, d - 4)
            )
            out.append(
                pltpu.make_async_remote_copy(
                    src_ref=source.at[x, k],
                    dst_ref=landing.at[x, k],
                    send_sem=send_sem.at[x, d],
                    recv_sem=recv_sem.at[x, d],
                    device_id=targets[d],
                    device_id_type=MESH,
                )
            )
        return out

    def block(r, c):
        return pl.ds(pl.multiple_of((r * wide + c) * TILE, TILE), TILE)

    def run(r, c, count):
        return pl.ds(pl.multiple_of((r * wide + c) * TILE, TILE), count * TILE)

    def send(x):
        send_edge[x, 0] = state[run(rows, 1, cols), :]
        send_edge[x, 1] = state[run(1, 1, cols), :]
        for r in range(rows):
            send_edge[x, 2, r * TILE : (r + 1) * TILE] = state[block(r + 1, cols), :]
            send_edge[x, 3, r * TILE : (r + 1) * TILE] = state[block(r + 1, 1), :]
        send_corner[x, 0] = state[block(rows, cols), :]
        send_corner[x, 1] = state[block(rows, 1), :]
        send_corner[x, 2] = state[block(1, cols), :]
        send_corner[x, 3] = state[block(1, 1), :]
        for copy, there in zip(copies(x), present):

            @pl.when(there)
            def _():
                copy.start()


    def receive(x):
        for d, copy in enumerate(copies(x)):

            @pl.when(present[opposite[d]])
            def _():
                copy.wait_recv()

        def kept(landed, d):
            return jnp.where(present[opposite[d]], landed, 0.0)

        state[run(0, 1, cols), :] = kept(land_edge[x, 0], 0)
        state[run(rows + 1, 1, cols), :] = kept(land_edge[x, 1], 1)
        for r in range(rows):
            part = slice(r * TILE, (r + 1) * TILE)
            state[block(r + 1, 0), :] = kept(land_edge[x, 2, part], 2)
            state[block(r + 1, cols + 1), :] = kept(land_edge[x, 3, part], 3)
        state[block(0, 0), :] = kept(land_corner[x, 0], 4)
        state[block(0, cols + 1), :] = kept(land_corner[x, 1], 5)
        state[block(rows + 1, 0), :] = kept(land_corner[x, 2], 6)
        state[block(rows + 1, cols + 1), :] = kept(land_corner[x, 3], 7)

    pl.semaphore_wait(barrier, sum(jnp.where(there, 1, 0) for there in present))
    send(0)

    def features(n):
        tile = state[pl.ds(pl.multiple_of(n * TILE, TILE), 8), :]
        x = jnp.where(row8 < 3, tile - centre, tile)
        norm = jnp.sum(jnp.where(row8 < 3, x * x, 0.0), axis=0, keepdims=True)
        radius = tile[3:4]
        x = jnp.where(row8 == 3, norm, jnp.where(row8 == 4, 1.0, x))
        h, m, l = pieces(x)
        zero = jnp.zeros_like(h)
        seen = jnp.where(row8 == 0, jnp.where(radius > 0.0, radius, absent), 0.0)
        moved = flat_rows(h, m, l)
        moved = jnp.where(row8 == 6, 1.0, moved)
        turned = jnp.transpose(
            jnp.concatenate([h, h, m, h, l, m, moved, zero + 1.0, seen] + [zero] * 7, axis=0)
        )
        left[n] = turned.astype(bf16)
        radb[n] = jnp.broadcast_to(turned[:, 64:65], (128, 128))
        v = jnp.concatenate([h, m, l, zero], axis=0).astype(bf16)
        value[n] = jnp.concatenate([v, v], axis=1)

    def flat_rows(h, m, l):
        out = jnp.zeros_like(h)
        for k, part in enumerate((h, m, l)):
            out = jnp.where(row8 == k, part[0:1], out)
            out = jnp.where(row8 == k + 3, part[1:2], out)
        return out

    lane8 = lax.broadcasted_iota(jnp.int32, (TILE, 128), 1)
    row32 = lax.broadcasted_iota(jnp.int32, (32, 256), 0)

    def partners(a, b):
        n = (a + 1) * wide + b + 1
        out = [(n, None, None, None)]
        for e in range(near):
            at = (a * cols + b) * near + e
            picked = listed[at]
            offset = jnp.where(picked >= 4, picked + 1, picked)
            u = jnp.where(offset >= 6, 1, jnp.where(offset >= 3, 0, -1))
            v = offset - 3 * (u + 1) - 1
            off = jnp.where(masked[at] > 0, 0.0, absent)
            out.append((n + u * wide + v, u.astype(f32), v.astype(f32), off))
        return out

    def squares(a, b):
        n = (a + 1) * wide + b + 1
        tile = state[pl.ds(pl.multiple_of(n * TILE, TILE), 8), :]
        x = jnp.where(row8 < 3, tile - centre, 0.0)
        norm = jnp.sum(x * x, axis=0, keepdims=True)
        y = jnp.where(row8 < 3, -2.0 * x, jnp.where(row8 == 3, 1.0, 0.0))
        y = jnp.where(row8 == 4, norm, y)
        h, m, l = pieces(y)
        two = jnp.where(row8 < 6, 2.0, jnp.where(row8 == 6, 1.0, 0.0))
        right = jnp.concatenate([h, m, h, l, h, m, two, flat_rows(h, m, l)], axis=0).astype(bf16)
        far = []
        for m, u, v, _ in partners(a, b):
            if u is None:
                scale = jnp.where(lane8 < 48, 1.0, 0.0)
            else:
                scale = jnp.where(lane8 < 48, 1.0, u)
                scale = jnp.where((lane8 >= 51) & (lane8 < 54), v, scale)
                scale = jnp.where(lane8 == 54, u * u + v * v, scale)
                scale = jnp.where(lane8 >= 59, v, scale)
            scale = jnp.concatenate([scale.astype(bf16)] * (128 // TILE), axis=0)
            far.append((left[m] * scale)[:, 0:64])
        far = jnp.concatenate(far, axis=0)
        return jnp.dot(far, right, preferred_element_type=f32)

    def overlaps(a, b, square):
        n = (a + 1) * wide + b + 1
        radius = state[pl.ds(pl.multiple_of(n * TILE, TILE), 8), :][3:4]
        weights, values = [], []
        for e, (m, u, v, off) in enumerate(partners(a, b)):
            row_radius = radius if off is None else radius + off
            part = jnp.maximum(square[e * 128 : (e + 1) * 128], floor_square)
            over = lax.rsqrt(part)
            s = jnp.maximum((radb[m] + row_radius) - part * over, 0.0)
            q = s * over
            s_high, q_high = s.astype(bf16), q.astype(bf16)
            s_low = (s - s_high.astype(f32)).astype(bf16)
            q_low = (q - q_high.astype(f32)).astype(bf16)
            weights.append(jnp.concatenate([s_high, q_high], axis=1))
            weights.append(jnp.concatenate([s_low, q_low], axis=1))
            mine = value[m]
            if u is not None:
                shift = jnp.where(row32 == 12, u, jnp.where(row32 == 20, v, 0.0))
                mine = mine + shift.astype(bf16)
            values.append(mine)
        return jnp.concatenate(values, axis=1), jnp.concatenate(weights, axis=0)

    def advance(step, a, b, sums):
        n = (a + 1) * wide + b + 1
        here = pl.ds(pl.multiple_of(n * TILE, TILE), TILE)
        tile = state[here, :]
        radius = tile[3:4]
        row3 = lax.broadcasted_iota(jnp.int32, (3, 128), 0)
        joined = sums[0:8] + sums[8:16] + sums[16:24]
        shift = jnp.where(row3 == 0, sums[12:13, 128:], jnp.where(row3 == 1, sums[20:21, 128:], 0.0))
        push = joined[0:3, 128:] + shift - (tile[0:3] - centre) * sums[4:5, 128:]
        load = tile[5:8] * sums[4:5, :128] - joined[5:8, :128]
        force = -normal_stiff * push - shear_stiff * load
        lift = normal_stiff * jnp.maximum(radius - tile[2:3], 0.0)
        force = force + jnp.where(row3 == 2, lift, 0.0)
        ratio = radius / base_radius
        speed = tile[8:11]
        wind = drag[pl.ds(pl.multiple_of((a * cols + b) * 8, 8), 8), :][0:3]
        accel = (
            force / (ratio * ratio * ratio)
            + drag_rate * (wind - speed)
            - jnp.where(row3 == 2, gravity, 0.0)
        )
        speed = speed + time_step * accel
        moved = tile[0:3] + time_step * speed
        spring = tile[5:8] + time_step * speed
        back = inv[step, a, pl.ds(b, 1), :].astype(f32)
        slots = slot[step, a, pl.ds(b, 1), :].astype(f32)
        state[here, :] = jnp.concatenate(
            [moved, radius, back, spring, speed, slots, tile[12:16]], axis=0
        )

    def spread(rows_of, count):
        one = rows_of.reshape(count, 1, 128)
        return jnp.broadcast_to(one, (count, TILE, 128))

    def make_packets(r, c, count):
        tiles = state[run(r, c, count), :].reshape(count, TILE, 128)
        index = spread(tiles[:, 11:12, :], count).astype(jnp.int32).reshape(count * TILE, 128)
        packet[run(r, c, count), :] = jnp.take_along_axis(
            tiles.reshape(count * TILE, 128), index, axis=1, mode="promise_in_bounds"
        )

    def trade(r, c, count, open_x, open_y):
        shape = (count, TILE, 128)
        up = packet[run(jnp.minimum(r + 1, high - 1), c, count), :].reshape(shape)
        down = packet[run(jnp.maximum(r - 1, 0), c, count), :].reshape(shape)
        if c == 0:
            line = packet[run(r, 0, count), :].reshape(shape)
            ahead = jnp.concatenate([line[1:], line[:1]], axis=0)
            behind = jnp.concatenate([line[-1:], line[:-1]], axis=0)
        else:
            ahead = packet[run(r, c + 1, count), :].reshape(shape)
            behind = packet[run(r, c - 1, count), :].reshape(shape)
        lane = lax.broadcasted_iota(jnp.int32, shape, 2)
        line_no = lax.broadcasted_iota(jnp.int32, shape, 1)
        column = lax.broadcasted_iota(jnp.int32, shape, 0) + c
        shift = jnp.where(
            lane < 32,
            jnp.where(line_no == 0, jnp.where(lane < 16, 1.0, -1.0), 0.0),
            jnp.where(line_no == 1, jnp.where(lane < 48, 1.0, -1.0), 0.0),
        )
        arriving = jnp.where(
            lane < 32, jnp.where(lane < 16, up, down), jnp.where(lane < 48, ahead, behind)
        )
        arriving = (arriving + shift).reshape(count * TILE, 128)
        tiles = state[run(r, c, count), :].reshape(shape)
        back = spread(tiles[:, 4:5, :], count).astype(jnp.int32)
        index = jnp.maximum(back, 0).reshape(count * TILE, 128)
        found = jnp.take_along_axis(arriving, index, axis=1, mode="promise_in_bounds")
        flag_y0, flag_y1 = open_y(column)
        allowed = jnp.where(
            back < 32,
            jnp.where(back < 16, open_x[0], open_x[1]),
            jnp.where(back < 48, flag_y0, flag_y1),
        )
        allowed = jnp.where((back >= 0) & (line_no != 4) & (line_no != 11), allowed, 0)
        state[run(r, c, count), :] = jnp.where(
            allowed > 0, found.reshape(shape), tiles
        ).reshape(count * TILE, 128)

    def as_int(flag):
        return jnp.where(flag, 1, 0)

    def features_of(first_row, last_row, columns):
        def feature_row(r, _):
            for c in columns:
                features(r * wide + c)
            return 0

        lax.fori_loop(first_row, last_row, feature_row, 0)

    def advance_blocks(step, group):
        apart = [squares(*at) for at in group]
        pairs = [overlaps(*at, square) for at, square in zip(group, apart)]
        sums = [jnp.dot(v, w, preferred_element_type=f32) for v, w in pairs]
        for at, total in zip(group, sums):
            advance(step, *at, total)

    def cross():
        make_packets(0, 0, wide)
        make_packets(rows + 1, 0, wide)

        def side_row(r, _):
            make_packets(r, 0, 1)
            make_packets(r, cols + 1, 1)
            return 0

        lax.fori_loop(1, rows + 1, side_row, 0)
        behind_x_open, ahead_x_open = as_int(has_behind_x), as_int(has_ahead_x)
        behind_y_open, ahead_y_open = as_int(has_behind_y), as_int(has_ahead_y)

        def cross_row(r, _):
            plus = jnp.where(r == 0, behind_x_open, jnp.where(r == rows, ahead_x_open, 0))
            minus = jnp.where(r == 1, behind_x_open, jnp.where(r == rows + 1, ahead_x_open, 0))

            def open_y(column):
                return (
                    jnp.where(
                        column == 0, behind_y_open, jnp.where(column == cols, ahead_y_open, 0)
                    ),
                    jnp.where(
                        column == 1, behind_y_open, jnp.where(column == cols + 1, ahead_y_open, 0)
                    ),
                )

            trade(r, 0, wide, (plus, minus), open_y)
            return 0

        lax.fori_loop(0, high, cross_row, 0)

    def substep(step, _):
        features_of(2, rows, range(2, cols))

        def advance_inner(i, _):
            for c in range(2, cols - 2, 4):
                advance_blocks(step, [(i + 2, c + k) for k in range(4)])
            return 0

        lax.fori_loop(0, rows - 4, advance_inner, 0)
        receive(step)

        @pl.when(step > 0)
        def _():
            cross()

        features_of(0, 2, range(wide))
        features_of(rows, rows + 2, range(wide))
        features_of(2, rows, (0, 1, cols, cols + 1))
        fours = cols // 4

        def advance_ends(i, _):
            r = i // fours
            a = r + (rows - 4) * (r // 2)
            advance_blocks(step, [(a, (i - r * fours) * 4 + k) for k in range(4)])
            return 0

        def advance_sides(i, _):
            advance_blocks(step, [(i + 2, b) for b in (0, 1, cols - 2, cols - 1)])
            return 0

        lax.fori_loop(0, 4 * fours, advance_ends, 0)
        lax.fori_loop(0, rows - 4, advance_sides, 0)

        def packets_row(r, _):
            make_packets(r, 1, cols)
            return 0

        lax.fori_loop(1, rows + 1, packets_row, 0)

        def inner_row(r, _):
            trade(
                r, 1, cols, (as_int(r < rows), as_int(r > 1)),
                lambda column: (as_int(column < cols), as_int(column > 1)),
            )
            return 0

        lax.fori_loop(1, rows + 1, inner_row, 0)
        send(step + 1)
        return 0

    lax.fori_loop(0, steps, substep, 0)
    receive(steps)
    cross()

    def store_row(a, _):
        first = ((a + 1) * wide + 1) * TILE
        for c in range(3):
            pos_out[c, a] = state[pl.ds(first + c, cols, stride=TILE), :]
            his_out[c, a] = state[pl.ds(first + 5 + c, cols, stride=TILE), :]
            vel_out[c, a] = state[pl.ds(first + 8 + c, cols, stride=TILE), :]
        return 0

    lax.fori_loop(0, rows, store_row, 0)

    def drain(x, _):
        for copy, there in zip(copies(x), present):

            @pl.when(there)
            def _():
                copy.wait_send()

        return 0

    lax.fori_loop(0, steps + 1, drain, 0)


def on_device(position, velocity, history, radius, fluid, tile_list, tile_mask, move_slot):
    size_x, size_y = lax.axis_size("gx"), lax.axis_size("gy")
    rows, cols, grains = radius.shape
    steps, near = move_slot.shape[0], tile_list.shape[-1]
    count = move_slot.shape[-1] // 4
    order = jnp.arange(4 * count, dtype=jnp.int32)
    hit = move_slot[..., :, None] == jnp.arange(grains, dtype=jnp.int32)
    inverse = jnp.sum(jnp.where(hit, order[:, None] + 1, 0), axis=-2) - 1
    groups = [move_slot[..., k * count : (k + 1) * count] for k in (1, 0, 3, 2)]
    slots = jnp.concatenate(groups + [jnp.zeros_like(move_slot)], axis=-1)
    blocks = (rows + 2) * (cols + 2)
    shape = jax.ShapeDtypeStruct(position.shape, f32)
    vmem = pl.BlockSpec(memory_space=pltpu.VMEM)
    smem = pl.BlockSpec(memory_space=pltpu.SMEM)
    return pl.pallas_call(
        functools.partial(kernel, (size_x, size_y, rows, cols, steps, near)),
        out_shape=(shape, shape, shape),
        in_specs=[vmem] * 7 + [smem] * 2,
        out_specs=(vmem, vmem, vmem),
        scratch_shapes=[
            pltpu.VMEM((blocks * TILE, grains), f32),
            pltpu.VMEM((blocks * TILE, grains), f32),
            pltpu.VMEM((blocks, 128, 128), bf16),
            pltpu.VMEM((blocks, 32, 256), bf16),
            pltpu.VMEM((blocks, 128, 128), f32),
            pltpu.VMEM((rows * cols * 8, grains), f32),
            pltpu.VMEM((steps + 1, 4, max(rows, cols) * TILE, grains), f32),
            pltpu.VMEM((steps + 1, 4, max(rows, cols) * TILE, grains), f32),
            pltpu.VMEM((steps + 1, 4, TILE, grains), f32),
            pltpu.VMEM((steps + 1, 4, TILE, grains), f32),
            pltpu.SemaphoreType.DMA((steps + 1, 8)),
            pltpu.SemaphoreType.DMA((steps + 1, 8)),
        ],
        compiler_params=pltpu.CompilerParams(
            collective_id=0, has_side_effects=True, vmem_limit_bytes=40 * 1024 * 1024
        ),
    )(
        position, velocity, history, radius, fluid, slots, inverse,
        tile_list.reshape(-1), tile_mask.reshape(-1),
    )


def solution(mesh):
    grid = P(None, "gx", "gy", None)
    flat = P("gx", "gy", None)
    return jax.shard_map(
        on_device,
        mesh=mesh,
        in_specs=(grid, grid, grid, flat, grid, flat, flat, grid),
        out_specs=(grid, grid, grid),
        check_vma=False,
    )
```

```python
import functools

import jax
import jax.numpy as jnp
from jax import lax
from jax.experimental import pallas as pl
from jax.experimental.pallas import tpu as pltpu
from jax.sharding import PartitionSpec as P

time_step = 0.05
normal_stiff = 50.0
shear_stiff = 40.0
drag_rate = 2.0
gravity = 1.0
floor_square = 0.0025
base_radius = 0.075
centre = 0.5
absent = -1.0e9
TILE = 16
MESH = pl.DeviceIdType.MESH
f32 = jnp.float32
bf16 = jnp.bfloat16


def pieces(x):
    high = x.astype(bf16).astype(f32)
    rest = x - high
    mid = rest.astype(bf16).astype(f32)
    low = (rest - mid).astype(bf16).astype(f32)
    return high, mid, low


def kernel(
    sizes, pos, vel, his, rad, fluid, slot, inv, listed, masked, pos_out, vel_out, his_out,
    state, packet, left, value, radb, drag, send_edge, land_edge, send_corner, land_corner,
    send_sem, recv_sem,
):
    size_x, size_y, rows, cols, steps, near = sizes
    wide = cols + 2
    high = rows + 2
    me_x = lax.axis_index("gx")
    me_y = lax.axis_index("gy")
    ahead_x, behind_x = lax.rem(me_x + 1, size_x), lax.rem(me_x + size_x - 1, size_x)
    ahead_y, behind_y = lax.rem(me_y + 1, size_y), lax.rem(me_y + size_y - 1, size_y)
    targets = [
        (ahead_x, me_y), (behind_x, me_y), (me_x, ahead_y), (me_x, behind_y),
        (ahead_x, ahead_y), (ahead_x, behind_y), (behind_x, ahead_y), (behind_x, behind_y),
    ]
    has_ahead_x, has_behind_x = me_x < size_x - 1, me_x > 0
    has_ahead_y, has_behind_y = me_y < size_y - 1, me_y > 0

    barrier = pltpu.get_barrier_semaphore()
    present = [
        has_ahead_x, has_behind_x, has_ahead_y, has_behind_y,
        has_ahead_x & has_ahead_y, has_ahead_x & has_behind_y,
        has_behind_x & has_ahead_y, has_behind_x & has_behind_y,
    ]
    opposite = [1, 0, 3, 2, 7, 6, 5, 4]
    for target, there in zip(targets, present):

        @pl.when(there)
        def _():
            pl.semaphore_signal(barrier, inc=1, device_id=target, device_id_type=MESH)


    row8 = lax.broadcasted_iota(jnp.int32, (8, 128), 0)

    def load_row(a, _):
        first = ((a + 1) * wide + 1) * TILE
        for c in range(3):
            state[pl.ds(first + c, cols, stride=TILE), :] = pos[c, a]
            state[pl.ds(first + 5 + c, cols, stride=TILE), :] = his[c, a]
            state[pl.ds(first + 8 + c, cols, stride=TILE), :] = vel[c, a]
            drag[pl.ds(a * cols * 8 + c, cols, stride=8), :] = fluid[c, a]
        state[pl.ds(first + 3, cols, stride=TILE), :] = rad[a]
        zero = jnp.zeros((cols, 128), f32)
        for c in (4, 11, 12, 13, 14, 15):
            state[pl.ds(first + c, cols, stride=TILE), :] = zero
        return 0

    lax.fori_loop(0, rows, load_row, 0)

    def copies(x):
        out = []
        for d in range(8):
            source, landing, k = (
                (send_edge, land_edge, d) if d < 4 else (send_corner, land_corner, d - 4)
            )
            out.append(
                pltpu.make_async_remote_copy(
                    src_ref=source.at[x, k],
                    dst_ref=landing.at[x, k],
                    send_sem=send_sem.at[x, d],
                    recv_sem=recv_sem.at[x, d],
                    device_id=targets[d],
                    device_id_type=MESH,
                )
            )
        return out

    def block(r, c):
        return pl.ds(pl.multiple_of((r * wide + c) * TILE, TILE), TILE)

    def run(r, c, count):
        return pl.ds(pl.multiple_of((r * wide + c) * TILE, TILE), count * TILE)

    def send(x):
        send_edge[x, 0] = state[run(rows, 1, cols), :]
        send_edge[x, 1] = state[run(1, 1, cols), :]
        for r in range(rows):
            send_edge[x, 2, r * TILE : (r + 1) * TILE] = state[block(r + 1, cols), :]
            send_edge[x, 3, r * TILE : (r + 1) * TILE] = state[block(r + 1, 1), :]
        send_corner[x, 0] = state[block(rows, cols), :]
        send_corner[x, 1] = state[block(rows, 1), :]
        send_corner[x, 2] = state[block(1, cols), :]
        send_corner[x, 3] = state[block(1, 1), :]
        for copy, there in zip(copies(x), present):

            @pl.when(there)
            def _():
                copy.start()


    def receive(x):
        for d, copy in enumerate(copies(x)):

            @pl.when(present[opposite[d]])
            def _():
                copy.wait_recv()

        def kept(landed, d):
            return jnp.where(present[opposite[d]], landed, 0.0)

        state[run(0, 1, cols), :] = kept(land_edge[x, 0], 0)
        state[run(rows + 1, 1, cols), :] = kept(land_edge[x, 1], 1)
        for r in range(rows):
            part = slice(r * TILE, (r + 1) * TILE)
            state[block(r + 1, 0), :] = kept(land_edge[x, 2, part], 2)
            state[block(r + 1, cols + 1), :] = kept(land_edge[x, 3, part], 3)
        state[block(0, 0), :] = kept(land_corner[x, 0], 4)
        state[block(0, cols + 1), :] = kept(land_corner[x, 1], 5)
        state[block(rows + 1, 0), :] = kept(land_corner[x, 2], 6)
        state[block(rows + 1, cols + 1), :] = kept(land_corner[x, 3], 7)

    pl.semaphore_wait(barrier, sum(jnp.where(there, 1, 0) for there in present))
    send(0)

    def features(n):
        tile = state[pl.ds(pl.multiple_of(n * TILE, TILE), 8), :]
        x = jnp.where(row8 < 3, tile - centre, tile)
        norm = jnp.sum(jnp.where(row8 < 3, x * x, 0.0), axis=0, keepdims=True)
        radius = tile[3:4]
        x = jnp.where(row8 == 3, norm, jnp.where(row8 == 4, 1.0, x))
        h, m, l = pieces(x)
        zero = jnp.zeros_like(h)
        seen = jnp.where(row8 == 0, jnp.where(radius > 0.0, radius, absent), 0.0)
        moved = flat_rows(h, m, l)
        moved = jnp.where(row8 == 6, 1.0, moved)
        turned = jnp.transpose(
            jnp.concatenate([h, h, m, h, l, m, moved, zero + 1.0, seen] + [zero] * 7, axis=0)
        )
        left[n] = turned.astype(bf16)
        radb[n] = jnp.broadcast_to(turned[:, 64:65], (128, 128))
        v = jnp.concatenate([h, m, l, zero], axis=0).astype(bf16)
        value[n] = jnp.concatenate([v, v], axis=1)

    def flat_rows(h, m, l):
        out = jnp.zeros_like(h)
        for k, part in enumerate((h, m, l)):
            out = jnp.where(row8 == k, part[0:1], out)
            out = jnp.where(row8 == k + 3, part[1:2], out)
        return out

    lane8 = lax.broadcasted_iota(jnp.int32, (TILE, 128), 1)
    row32 = lax.broadcasted_iota(jnp.int32, (32, 256), 0)

    def partners(a, b):
        n = (a + 1) * wide + b + 1
        out = [(n, None, None, None)]
        for e in range(near):
            at = (a * cols + b) * near + e
            picked = listed[at]
            offset = jnp.where(picked >= 4, picked + 1, picked)
            u = jnp.where(offset >= 6, 1, jnp.where(offset >= 3, 0, -1))
            v = offset - 3 * (u + 1) - 1
            off = jnp.where(masked[at] > 0, 0.0, absent)
            out.append((n + u * wide + v, u.astype(f32), v.astype(f32), off))
        return out

    def squares(a, b):
        n = (a + 1) * wide + b + 1
        tile = state[pl.ds(pl.multiple_of(n * TILE, TILE), 8), :]
        x = jnp.where(row8 < 3, tile - centre, 0.0)
        norm = jnp.sum(x * x, axis=0, keepdims=True)
        y = jnp.where(row8 < 3, -2.0 * x, jnp.where(row8 == 3, 1.0, 0.0))
        y = jnp.where(row8 == 4, norm, y)
        h, m, l = pieces(y)
        two = jnp.where(row8 < 6, 2.0, jnp.where(row8 == 6, 1.0, 0.0))
        right = jnp.concatenate([h, m, h, l, h, m, two, flat_rows(h, m, l)], axis=0).astype(bf16)
        far = []
        for m, u, v, _ in partners(a, b):
            if u is None:
                scale = jnp.where(lane8 < 48, 1.0, 0.0)
            else:
                scale = jnp.where(lane8 < 48, 1.0, u)
                scale = jnp.where((lane8 >= 51) & (lane8 < 54), v, scale)
                scale = jnp.where(lane8 == 54, u * u + v * v, scale)
                scale = jnp.where(lane8 >= 59, v, scale)
            scale = jnp.concatenate([scale.astype(bf16)] * (128 // TILE), axis=0)
            far.append((left[m] * scale)[:, 0:64])
        far = jnp.concatenate(far, axis=0)
        return jnp.dot(far, right, preferred_element_type=f32)

    def overlaps(a, b, square):
        n = (a + 1) * wide + b + 1
        radius = state[pl.ds(pl.multiple_of(n * TILE, TILE), 8), :][3:4]
        weights, values = [], []
        for e, (m, u, v, off) in enumerate(partners(a, b)):
            row_radius = radius if off is None else radius + off
            part = jnp.maximum(square[e * 128 : (e + 1) * 128], floor_square)
            over = lax.rsqrt(part)
            s = jnp.maximum((radb[m] + row_radius) - part * over, 0.0)
            q = s * over
            s_high, q_high = s.astype(bf16), q.astype(bf16)
            s_low = (s - s_high.astype(f32)).astype(bf16)
            q_low = (q - q_high.astype(f32)).astype(bf16)
            weights.append(jnp.concatenate([s_high, q_high], axis=1))
            weights.append(jnp.concatenate([s_low, q_low], axis=1))
            mine = value[m]
            if u is not None:
                shift = jnp.where(row32 == 12, u, jnp.where(row32 == 20, v, 0.0))
                mine = mine + shift.astype(bf16)
            values.append(mine)
        return jnp.concatenate(values, axis=1), jnp.concatenate(weights, axis=0)

    def advance(step, a, b, sums):
        n = (a + 1) * wide + b + 1
        here = pl.ds(pl.multiple_of(n * TILE, TILE), TILE)
        tile = state[here, :]
        radius = tile[3:4]
        row3 = lax.broadcasted_iota(jnp.int32, (3, 128), 0)
        joined = sums[0:8] + sums[8:16] + sums[16:24]
        shift = jnp.where(row3 == 0, sums[12:13, 128:], jnp.where(row3 == 1, sums[20:21, 128:], 0.0))
        push = joined[0:3, 128:] + shift - (tile[0:3] - centre) * sums[4:5, 128:]
        load = tile[5:8] * sums[4:5, :128] - joined[5:8, :128]
        force = -normal_stiff * push - shear_stiff * load
        lift = normal_stiff * jnp.maximum(radius - tile[2:3], 0.0)
        force = force + jnp.where(row3 == 2, lift, 0.0)
        ratio = radius / base_radius
        speed = tile[8:11]
        wind = drag[pl.ds(pl.multiple_of((a * cols + b) * 8, 8), 8), :][0:3]
        accel = (
            force / (ratio * ratio * ratio)
            + drag_rate * (wind - speed)
            - jnp.where(row3 == 2, gravity, 0.0)
        )
        speed = speed + time_step * accel
        moved = tile[0:3] + time_step * speed
        spring = tile[5:8] + time_step * speed
        back = inv[step, a, pl.ds(b, 1), :].astype(f32)
        slots = slot[step, a, pl.ds(b, 1), :].astype(f32)
        state[here, :] = jnp.concatenate(
            [moved, radius, back, spring, speed, slots, tile[12:16]], axis=0
        )

    lane = lax.broadcasted_iota(jnp.int32, (8, 128), 1)
    shift = jnp.where(
        lane < 32,
        jnp.where(row8 == 0, jnp.where(lane < 16, 1.0, -1.0), 0.0),
        jnp.where(row8 == 1, jnp.where(lane < 48, 1.0, -1.0), 0.0),
    )

    def half(n, k):
        return pl.ds(pl.multiple_of(n * TILE + 8 * k, 8), 8)

    def gather(x, index):
        return jnp.take_along_axis(x, index, axis=1, mode="promise_in_bounds")

    def make_packets(r, columns):
        out = []
        for c in columns:
            n = r * wide + c
            first, second = state[half(n, 0), :], state[half(n, 1), :]
            index = jnp.broadcast_to(second[3:4], (8, 128)).astype(jnp.int32)
            out.append((n, gather(first, index), gather(second, index)))
        for n, first, second in out:
            packet[half(n, 0), :] = first
            packet[half(n, 1), :] = second

    def trade(r, columns, flags):
        out = []
        for c in columns:
            n = r * wide + c
            sides = (
                jnp.minimum(r + 1, high - 1) * wide + c,
                jnp.maximum(r - 1, 0) * wide + c,
                r * wide + min(c + 1, wide - 1),
                r * wide + max(c - 1, 0),
            )
            first, second = state[half(n, 0), :], state[half(n, 1), :]
            back = jnp.broadcast_to(first[4:5], (8, 128)).astype(jnp.int32)
            moves = lax.shift_right_logical(
                jnp.broadcast_to(flags(c), (8, 128)), lax.shift_right_logical(back, 4)
            )
            moves = (moves & 1) > 0
            halves = []
            for k in range(2):
                come = [packet[half(side, k), :] for side in sides]
                come = jnp.where(
                    lane < 32,
                    jnp.where(lane < 16, come[0], come[1]),
                    jnp.where(lane < 48, come[2], come[3]),
                )
                halves.append(gather(come + shift if k == 0 else come, back))
            out.append(
                (
                    n,
                    jnp.where(moves & (row8 != 4), halves[0], first),
                    jnp.where(moves & (row8 != 3), halves[1], second),
                )
            )
        for n, first, second in out:
            state[half(n, 0), :] = first
            state[half(n, 1), :] = second

    def as_int(flag):
        return jnp.where(flag, 1, 0)

    def features_of(first_row, last_row, columns):
        def feature_row(r, _):
            for c in columns:
                features(r * wide + c)
            return 0

        lax.fori_loop(first_row, last_row, feature_row, 0)

    def advance_blocks(step, group):
        sums = []
        ahead = squares(*group[0])
        for k, at in enumerate(group):
            square = ahead
            if k + 1 < len(group):
                ahead = squares(*group[k + 1])
            mine, weights = overlaps(*at, square)
            sums.append(jnp.dot(mine, weights, preferred_element_type=f32))
        for at, total in zip(group, sums):
            advance(step, *at, total)

    def cross():
        make_packets(0, range(wide))
        make_packets(rows + 1, range(wide))

        def side_row(r, _):
            make_packets(r, (0, cols + 1))
            return 0

        lax.fori_loop(1, rows + 1, side_row, 0)
        behind_x_open, ahead_x_open = as_int(has_behind_x), as_int(has_ahead_x)
        behind_y_open, ahead_y_open = as_int(has_behind_y), as_int(has_ahead_y)

        def open_y(c):
            if c == 0:
                return 4 * behind_y_open
            if c == 1:
                return 8 * behind_y_open
            if c == cols:
                return 4 * ahead_y_open
            return 8 * ahead_y_open if c == cols + 1 else 0

        def end_rows(r, open_x):
            trade(r, range(wide), lambda c: open_x + open_y(c))

        end_rows(0, behind_x_open)
        end_rows(1, 2 * behind_x_open)
        end_rows(rows, ahead_x_open)
        end_rows(rows + 1, 2 * ahead_x_open)

        def side_rows(i, _):
            for k in range(2):
                trade(2 * i + 2 + k, (0, 1, cols, cols + 1), open_y)
            return 0

        lax.fori_loop(0, (rows - 2) // 2, side_rows, 0)

    def substep(step, _):
        features_of(2, rows, range(2, cols))

        def advance_inner(i, _):
            for c in range(2, cols - 2, 4):
                advance_blocks(step, [(i + 2, c + k) for k in range(4)])
            return 0

        lax.fori_loop(0, rows - 4, advance_inner, 0)
        receive(step)

        @pl.when(step > 0)
        def _():
            cross()

        features_of(0, 2, range(wide))
        features_of(rows, rows + 2, range(wide))
        features_of(2, rows, (0, 1, cols, cols + 1))
        fours = cols // 4

        def edge_ends(i, _):
            r = i // fours
            advance_blocks(step, [(r * (rows - 1), (i - r * fours) * 4 + k) for k in range(4)])
            return 0

        def edge_sides(i, _):
            advance_blocks(
                step, [(2 * i + 1 + j, b) for j in range(2) for b in (0, cols - 1)]
            )
            return 0

        def next_ends(i, _):
            advance_blocks(
                step, [(a, 2 * i + 1 + k) for a in (1, rows - 2) for k in range(2)]
            )
            return 0

        def next_sides(i, _):
            advance_blocks(
                step, [(2 * i + 2 + j, b) for j in range(2) for b in (1, cols - 2)]
            )
            return 0

        lax.fori_loop(0, 2 * fours, edge_ends, 0)
        lax.fori_loop(0, (rows - 2) // 2, edge_sides, 0)

        @pl.when(step == steps - 1)
        def _():
            send(step + 1)

        lax.fori_loop(0, (cols - 2) // 2, next_ends, 0)
        lax.fori_loop(0, (rows - 4) // 2, next_sides, 0)

        def packets_row(r, _):
            make_packets(r, range(1, cols + 1))
            return 0

        lax.fori_loop(1, rows + 1, packets_row, 0)

        def inner_row(r, _):
            open_x = as_int(r < rows) + 2 * as_int(r > 1)
            trade(
                r, range(1, cols + 1), lambda c: open_x + 4 * int(c < cols) + 8 * int(c > 1)
            )
            return 0

        lax.fori_loop(1, rows + 1, inner_row, 0)

        @pl.when(step < steps - 1)
        def _():
            send(step + 1)

        return 0

    lax.fori_loop(0, steps, substep, 0)
    receive(steps)
    cross()

    def store_row(a, _):
        first = ((a + 1) * wide + 1) * TILE
        for c in range(3):
            pos_out[c, a] = state[pl.ds(first + c, cols, stride=TILE), :]
            his_out[c, a] = state[pl.ds(first + 5 + c, cols, stride=TILE), :]
            vel_out[c, a] = state[pl.ds(first + 8 + c, cols, stride=TILE), :]
        return 0

    lax.fori_loop(0, rows, store_row, 0)

    def drain(x, _):
        for copy, there in zip(copies(x), present):

            @pl.when(there)
            def _():
                copy.wait_send()

        return 0

    lax.fori_loop(0, steps + 1, drain, 0)


def on_device(position, velocity, history, radius, fluid, tile_list, tile_mask, move_slot):
    size_x, size_y = lax.axis_size("gx"), lax.axis_size("gy")
    rows, cols, grains = radius.shape
    steps, near = move_slot.shape[0], tile_list.shape[-1]
    count = move_slot.shape[-1] // 4
    order = jnp.arange(4 * count, dtype=jnp.int32)
    hit = move_slot[..., :, None] == jnp.arange(grains, dtype=jnp.int32)
    inverse = jnp.sum(jnp.where(hit, order[:, None] - 4 * count, 0), axis=-2) + 4 * count
    groups = [move_slot[..., k * count : (k + 1) * count] for k in (1, 0, 3, 2)]
    slots = jnp.concatenate(groups + [jnp.zeros_like(move_slot)], axis=-1)
    blocks = (rows + 2) * (cols + 2)
    shape = jax.ShapeDtypeStruct(position.shape, f32)
    vmem = pl.BlockSpec(memory_space=pltpu.VMEM)
    smem = pl.BlockSpec(memory_space=pltpu.SMEM)
    return pl.pallas_call(
        functools.partial(kernel, (size_x, size_y, rows, cols, steps, near)),
        out_shape=(shape, shape, shape),
        in_specs=[vmem] * 7 + [smem] * 2,
        out_specs=(vmem, vmem, vmem),
        scratch_shapes=[
            pltpu.VMEM((blocks * TILE, grains), f32),
            pltpu.VMEM((blocks * TILE, grains), f32),
            pltpu.VMEM((blocks, 128, 128), bf16),
            pltpu.VMEM((blocks, 32, 256), bf16),
            pltpu.VMEM((blocks, 128, 128), f32),
            pltpu.VMEM((rows * cols * 8, grains), f32),
            pltpu.VMEM((steps + 1, 4, max(rows, cols) * TILE, grains), f32),
            pltpu.VMEM((steps + 1, 4, max(rows, cols) * TILE, grains), f32),
            pltpu.VMEM((steps + 1, 4, TILE, grains), f32),
            pltpu.VMEM((steps + 1, 4, TILE, grains), f32),
            pltpu.SemaphoreType.DMA((steps + 1, 8)),
            pltpu.SemaphoreType.DMA((steps + 1, 8)),
        ],
        compiler_params=pltpu.CompilerParams(
            collective_id=0, has_side_effects=True, vmem_limit_bytes=40 * 1024 * 1024
        ),
    )(
        position, velocity, history, radius, fluid, slots, inverse,
        tile_list.reshape(-1), tile_mask.reshape(-1),
    )


def solution(mesh):
    grid = P(None, "gx", "gy", None)
    flat = P("gx", "gy", None)
    return jax.shard_map(
        on_device,
        mesh=mesh,
        in_specs=(grid, grid, grid, flat, grid, flat, flat, grid),
        out_specs=(grid, grid, grid),
        check_vma=False,
    )
```
